256 devices in a mesh: replica: 64 (over z, y, x_lo), fsdp: 4 (over x_hi, core).
Axes of the slice: x: 4 (x_hi: 2, x_lo: 2; x = x_hi * 2 + x_lo), y: 4, z: 8, core: 2. Of those that a mesh axis runs over, the one named last changes fastest.
Arguments:
- tokens: bfloat16 [131072, 2048], P(('replica', 'fsdp')), may hold values from -30 to 30
- cotangent: bfloat16 [131072, 512], P(('replica', 'fsdp')), may hold values from -6 to 6
- step_count: int32 [1], replicated, may hold values from 1 to 8
- master: float32 [64, 512, 2048], P('replica', 'fsdp'), may hold values from -16 to 16
- first_moment_adamw: float32 [64, 512, 2048], P('replica', 'fsdp'), may hold values from -6 to 6
- moment_second: float32 [64, 512, 2048], P('replica', 'fsdp'), may hold values from 0.05 to 5
- anchor: float32 [512, 2048], P('fsdp', 'replica'), may hold values from -6 to 6
- outer_moment: float32 [512, 2048], P('fsdp', 'replica'), may hold values from -3 to 3
- pending: float32 [512, 2048], P('fsdp', 'replica'), may hold values from -3 to 3
Outputs:
- key_out: bfloat16 [131072, 512], P(('replica', 'fsdp'))
- input_grad: bfloat16 [131072, 2048], P(('replica', 'fsdp'))
- params: float32 [64, 512, 2048], P('replica', 'fsdp')
- moment_first_new: float32 [64, 512, 2048], P('replica', 'fsdp')
- moment_second_new: float32 [64, 512, 2048], P('replica', 'fsdp')
- anchor_new: float32 [512, 2048], P('fsdp', 'replica')
- outer_moment_new: float32 [512, 2048], P('fsdp', 'replica')
- pending_new: float32 [512, 2048], P('fsdp', 'replica')
The draws below stay inside these ranges and needn't reach their ends.
All inputs are finite; a program needn't handle non-finite values.
Results may differ from the reference program's by a relative error of at most 0.0058.
Values may be sent and summed in bfloat16 or wider, within the bound.
A program may use at most 64 MiB of HBM per device.

```python
import math
import jax
import jax.numpy as jnp
from jax import lax

MODEL_WIDTH = 2048
HEAD_DIM = 64
DEVICE_TOKENS = 512
KEY_FEATURES = 512
REPLICAS = 64
TOKENS = 131072
N_REPLICA = 64
N_FSDP = 4


def draw_tokens(key, part):
    key = jax.random.fold_in(key, 17)
    value_key, key_row_values, col_key = jax.random.split(key, 3)
    raw_values = jnp.clip(jax.random.normal(value_key, (TOKENS, MODEL_WIDTH), jnp.float32), -5.0, 5.0)
    row_low = 0.3
    row_high = 3.0
    row_scale = jnp.exp(jax.random.uniform(key_row_values, (TOKENS, 1), jnp.float32, math.log(row_low), math.log(row_high)))
    col_scale = jnp.exp(jax.random.uniform(col_key, (1, MODEL_WIDTH), jnp.float32, math.log(0.5), math.log(2.0)))
    return (raw_values * row_scale * col_scale).astype(jnp.bfloat16)


def raised(entries, key, source, target, blocks, factor):
    owner, partner = [(jnp.arange(entries.shape[position]) // (entries.shape[position] // blocks)).reshape([-1 if axis == position else 1 for axis in range(entries.ndim)]) for position in (source, target)]
    chosen = jax.random.permutation(key, blocks)[partner]
    strong = (owner == chosen) | (owner == (partner + blocks // 2) % blocks)
    return jnp.where(strong, factor * entries, entries)


def steps_of(stream_key, shape, cuts, smallest, top_value):
    gain = 1.0
    for dim, parts in cuts:
        steps = jax.random.uniform(jax.random.fold_in(jax.random.fold_in(stream_key, 6), dim), (parts,), jnp.float32, smallest / len(cuts), top_value / len(cuts))
        gain = gain * jnp.repeat(jnp.exp(steps), shape[dim] // parts).reshape((-1,) + (1,) * (len(shape) - 1 - dim))
    return gain


def centred(key, extent, deviation, most, cuts=(), dtype=jnp.bfloat16):
    drawn = jax.random.normal(key, extent, jnp.float32) * deviation
    if len(cuts) > 0:
        drawn = steps_of(key, extent, cuts, -0.22, 0.18) * drawn
    return jnp.clip(drawn, min=-most, max=most).astype(dtype)


def bell_draw_with(key, dims, width, limit, cuts, heavy, kind=jnp.bfloat16):
    values = width * jax.random.normal(key, dims, jnp.float32)
    if cuts:
        values = values * steps_of(key, dims, cuts, -0.22, 0.18)
    return jnp.clip(raised(values, jax.random.fold_in(key, 3), *heavy), -limit, limit).astype(kind)


def setup_inputs(seed: int = 0) -> dict:
    arg_keys = jax.random.split(jax.random.key(seed), 10)
    tokens = draw_tokens(jax.random.fold_in(arg_keys[9], 71), 0)
    cotangent = centred(arg_keys[1], (TOKENS, KEY_FEATURES), 1.0, 6.0, ((0, 256),))
    step_count = jax.random.randint(arg_keys[2], (1,), 1, 9).astype(jnp.int32)
    master = bell_draw_with(arg_keys[3], (REPLICAS, KEY_FEATURES, MODEL_WIDTH), 1.0, 16.0, ((0, 64), (1, 4)), (0, 2, 64, 4.0), jnp.float32)
    first_moment_adamw = centred(arg_keys[4], (REPLICAS, KEY_FEATURES, MODEL_WIDTH), 1.0, 6.0, ((0, 64), (1, 4)), jnp.float32)
    moment_second = jnp.clip(jnp.exp(math.log(5.0) - 4.6051702 * jax.random.uniform(arg_keys[5], (REPLICAS, KEY_FEATURES, MODEL_WIDTH), jnp.float32) ** steps_of(arg_keys[5], (REPLICAS, KEY_FEATURES, MODEL_WIDTH), ((0, 64), (1, 4)), -0.2, 0.2)), 0.05, 5.0)
    anchor = centred(arg_keys[6], (KEY_FEATURES, MODEL_WIDTH), 1.0, 6.0, ((0, 4), (1, 64)), jnp.float32)
    outer_moment = centred(arg_keys[7], (KEY_FEATURES, MODEL_WIDTH), 0.5, 3.0, ((0, 4), (1, 64)), jnp.float32)
    pending = centred(arg_keys[8], (KEY_FEATURES, MODEL_WIDTH), 0.5, 3.0, ((0, 4), (1, 64)), jnp.float32)
    return {"tokens": tokens, "cotangent": cotangent, "step_count": step_count, "master": master, "first_moment_adamw": first_moment_adamw, "moment_second": moment_second, "anchor": anchor, "outer_moment": outer_moment, "pending": pending}


ROPE_BASE = 500000.0
EPS_NORM = 1e-05
BETA_ONE = 0.9
BETA_TWO = 0.95
EPS_ADAM = 1e-08
LEARN_RATE = 0.1
WEIGHT_DECAY = 0.1
OUTER_RATE = 0.7
OUTER_MOMENTUM = 0.9
MIX_LOCAL = 0.5

def rope_tables(positions, col_count, head_size):
    column = jnp.arange(col_count) % head_size % (head_size // 2)
    exponent = 2.0 * column.astype(jnp.float32) / head_size
    inverse_freq = jnp.exp(-exponent * math.log(ROPE_BASE))
    angles = positions[:, None] * inverse_freq[None, :]
    return (jnp.cos(angles), jnp.sin(angles))

def rotate_half(values, head_size):
    row_count, col_count = values.shape
    halves = values.reshape(row_count, col_count // head_size, 2, head_size // 2)
    turned = jnp.concatenate([-halves[:, :, 1:2], halves[:, :, 0:1]], axis=2)
    return turned.reshape(row_count, col_count)

def norm_forward(tokens):
    floats = tokens.astype(jnp.float32)
    inverse = lax.rsqrt(lax.optimization_barrier(jnp.mean(floats * floats, axis=-1, keepdims=True)) + EPS_NORM)
    return (floats, inverse)

def norm_backward(floats, inverse, hidden_grad):
    inner_sum = lax.optimization_barrier(jnp.mean(hidden_grad * floats, axis=-1, keepdims=True))
    return (inverse * hidden_grad - floats * inverse ** 3 * inner_sum).astype(jnp.bfloat16)

def adam_update(weights, gradient, moment_one, moment_two, bias_one, bias_two):
    moment_one_new = BETA_ONE * moment_one + (1.0 - BETA_ONE) * gradient
    moment_two_new = BETA_TWO * moment_two + (1.0 - BETA_TWO) * gradient * gradient
    update = moment_one_new / bias_one / (jnp.sqrt(moment_two_new / bias_two) + EPS_ADAM)
    return (weights - LEARN_RATE * (update + WEIGHT_DECAY * weights), moment_one_new, moment_two_new)

def outer_merge(anchor, outer_moment, pending):
    outer_moment_new = OUTER_MOMENTUM * outer_moment + pending
    anchor_new = anchor - OUTER_RATE * (pending + OUTER_MOMENTUM * outer_moment_new)
    return (anchor_new, outer_moment_new)

def reference(tokens, cotangent, step_count, master, first_moment_adamw, moment_second, anchor, outer_moment, pending):
    per_replica = DEVICE_TOKENS * N_FSDP
    scale_factor = 1.0 / math.sqrt(MODEL_WIDTH)
    positions = (jnp.arange(per_replica) % DEVICE_TOKENS).astype(jnp.float32)
    cosine, sine_table = rope_tables(positions, KEY_FEATURES, HEAD_DIM)
    steps_float = step_count[0].astype(jnp.float32)
    bias_one = 1.0 - jnp.power(jnp.float32(BETA_ONE), steps_float)
    bias_two = 1.0 - jnp.power(jnp.float32(BETA_TWO), steps_float)

    def one_replica(pieces):
        block_tokens, block_cot, weights_full, moment_one, moment_two = pieces
        floats, inverse = norm_forward(block_tokens)
        normalized_input = (floats * inverse).astype(jnp.bfloat16)
        weights_half = weights_full.astype(jnp.bfloat16)
        projected = jnp.dot(normalized_input, weights_half.T, preferred_element_type=jnp.float32) * scale_factor
        key_out = (projected * cosine + rotate_half(projected, HEAD_DIM) * sine_table).astype(jnp.bfloat16)
        cot_float = block_cot.astype(jnp.float32)
        key_gradient = ((cot_float * cosine - rotate_half(cot_float * sine_table, HEAD_DIM)) * scale_factor).astype(jnp.bfloat16)
        hidden_grad = jnp.dot(key_gradient, weights_half, preferred_element_type=jnp.float32)
        input_grad = norm_backward(floats, inverse, hidden_grad)
        gradient_block_list = jnp.einsum('ngy,ngf->nyf', key_gradient.reshape(N_FSDP, DEVICE_TOKENS, KEY_FEATURES).astype(jnp.float32), normalized_input.reshape(N_FSDP, DEVICE_TOKENS, MODEL_WIDTH).astype(jnp.float32), precision=lax.Precision.HIGHEST)
        rounded = lax.optimization_barrier(gradient_block_list.astype(jnp.bfloat16))
        gradient = lax.optimization_barrier(jnp.sum(rounded.astype(jnp.float32), axis=0))
        inner, moment_one_new, moment_two_new = adam_update(weights_full, gradient, moment_one, moment_two, bias_one, bias_two)
        return (key_out, input_grad, inner, moment_one_new, moment_two_new)
    results = lax.map(one_replica, (tokens.reshape(N_REPLICA, per_replica, MODEL_WIDTH), cotangent.reshape(N_REPLICA, per_replica, KEY_FEATURES), master, first_moment_adamw, moment_second))
    key_out, input_grad, inner, moment_first_new, moment_second_new = results
    anchor_new, outer_moment_new = outer_merge(anchor, outer_moment, pending)
    pending_new = anchor - lax.optimization_barrier(jnp.sum(inner, axis=0)) / N_REPLICA
    params = MIX_LOCAL * inner + (1.0 - MIX_LOCAL) * anchor_new[None]
    return (key_out.reshape(TOKENS, KEY_FEATURES), input_grad.reshape(TOKENS, MODEL_WIDTH), params, moment_first_new, moment_second_new, anchor_new, outer_moment_new, pending_new)
```

```python
import math

import jax
import jax.numpy as jnp
import numpy as np
from jax import lax
from jax.experimental import pallas as pl
from jax.experimental.pallas import tpu as pltpu
from jax.sharding import PartitionSpec as P

MESH = pl.DeviceIdType.MESH
F32 = jnp.float32
BF16 = jnp.bfloat16

HEAD_DIM = 64
ROPE_BASE = 500000.0
EPS_NORM = 1e-05
BETA_ONE = 0.9
BETA_TWO = 0.95
EPS_ADAM = 1e-08
LEARN_RATE = 0.1
WEIGHT_DECAY = 0.1
OUTER_RATE = 0.7
OUTER_MOMENTUM = 0.9

TOK = 512
WIDTH = 2048
KEYS = 512
ROWS = 128
NZ, NY = 8, 4
CW = WIDTH // NZ
FEAT = 32
EARLY = 4
LAG = 3


def rope_tables():
    lane = np.arange(128)
    exponent = 2.0 * (lane % HEAD_DIM % (HEAD_DIM // 2)) / HEAD_DIM
    angles = np.arange(TOK)[:, None] * np.exp(-exponent * math.log(ROPE_BASE))[None, :]
    sign = np.where(lane % HEAD_DIM < HEAD_DIM // 2, -1.0, 1.0)[None, :]
    scale = 1.0 / math.sqrt(WIDTH)
    return (
        (np.cos(angles) * scale).astype(np.float32),
        (np.sin(angles) * sign * scale).astype(np.float32),
    )


def swap_halves(values):
    lane = lax.broadcasted_iota(jnp.int32, values.shape, 1)
    first = lax.rem(lane, HEAD_DIM) < HEAD_DIM // 2
    return jnp.where(first, pltpu.roll(values, 96, 1), pltpu.roll(values, 32, 1))


def step_kernel(
    stp, tok_h, cot_h, mas_h, m1_h, m2_h, anc_h, om_h, pen_h, cos_h, sin_h,
    tk, cs, sn, iv, pj, hd, acc, pv, m1n, m2n, smo,
    ct, ms, m1, m2, sm, nm, kg, kgt, wf, gb, rs, xs, xr, ib, rb, qs, qr, mt,
    ld,
    wss, wsr, wxs, wxr, wfs, wfr,
    gss, gsr, gxs, gxr, rzs, rzr, qss, qsr,
    a1, a2s, a2r, a3s, a3r,
):
    r = lax.axis_index("replica")
    f = lax.axis_index("fsdp")
    z = lax.div(r, 8)
    y = lax.rem(lax.div(r, 2), 4)
    xl = lax.rem(r, 2)
    core = lax.rem(f, 2)
    f_sib = f + 1 - 2 * core
    f_cross = lax.rem(f + 2, 4)
    f_diag = lax.rem(f_sib + 2, 4)
    sibling = (r, f_sib)
    cross = (r, f_cross)

    def at(zz, yy, xx):
        return ((zz * NY + yy) * 2 + xx, f)

    def z_peer(d):
        return lax.rem(z + d, NZ)

    def y_peer(d):
        return lax.rem(y + d, NY)

    def yx_peer(d):
        return y_peer(lax.div(d, 2)), lax.rem(xl + lax.rem(d, 2), 2)

    def chunk(i):
        half = lax.div(i + 1, 2)
        return lax.rem(z + 4 + (1 - 2 * lax.rem(i, 2)) * half, NZ)

    def rcopy(src, dst, send, recv, device):
        return pltpu.make_async_remote_copy(
            src_ref=src, dst_ref=dst, send_sem=send, recv_sem=recv,
            device_id=device, device_id_type=MESH,
        )

    def rank_rows(rank):
        return pl.ds(pl.multiple_of(rank * ROWS, ROWS), ROWS)

    def cols(c):
        return pl.ds(pl.multiple_of(c * CW, CW), CW)

    def w_sib(c, rank):
        block = wf.at[c, rank_rows(rank)]
        return rcopy(block, block, wss.at[c], wsr.at[c], sibling)

    def w_cross(c, rank):
        block = wf.at[c, rank_rows(rank)]
        return rcopy(block, block, wxs.at[c], wxr.at[c], cross)

    def w_fwd(c, rank):
        block = wf.at[c, rank_rows(rank)]
        return rcopy(block, block, wfs.at[c], wfr.at[c], sibling)

    def g_sib(c):
        return rcopy(
            gb.at[c, pl.ds(2 * ROWS, 2 * ROWS)], rs.at[c], gss.at[c], gsr.at[c], sibling
        )

    def g_cross(c):
        return rcopy(xs.at[c], xr.at[c], gxs.at[c], gxr.at[c], cross)

    def sum_z(c, slot):
        return rcopy(ib.at[c], rb.at[slot], rzs.at[c], rzr.at[slot], at(c, y, xl))

    def sum_yx(yy, xx, slot):
        part = yy * 2 + xx
        return rcopy(
            qs.at[pl.ds(pl.multiple_of(part * FEAT, FEAT), FEAT)], qr.at[slot],
            qss.at[part], qsr.at[slot], at(z, yy, xx),
        )

    def m_x(slot):
        block = mt.at[y, z, pl.ds(pl.multiple_of(slot * FEAT, FEAT), FEAT)]
        return rcopy(block, block, a1.at[0], a1.at[1], at(z, y, 1 - xl))

    def m_z(zz, slot):
        block = mt.at[y, slot]
        return rcopy(block, block, a2s.at[zz], a2r.at[slot], at(zz, y, xl))

    def m_y(yy, slot):
        block = mt.at[slot]
        return rcopy(block, block, a3s.at[yy], a3r.at[slot], at(z, yy, xl))

    loads = [
        pltpu.make_async_copy(mas_h, ms, ld.at[0]),
        pltpu.make_async_copy(anc_h, sm.at[0], ld.at[1]),
        pltpu.make_async_copy(om_h, sm.at[1], ld.at[2]),
        pltpu.make_async_copy(pen_h, sm.at[2], ld.at[3]),
        pltpu.make_async_copy(tok_h, tk, ld.at[4]),
        pltpu.make_async_copy(cot_h, ct, ld.at[5]),
        pltpu.make_async_copy(cos_h, cs, ld.at[6]),
        pltpu.make_async_copy(sin_h, sn, ld.at[7]),
        pltpu.make_async_copy(m1_h, m1, ld.at[8]),
        pltpu.make_async_copy(m2_h, m2, ld.at[9]),
    ]
    for load in loads:
        load.start()

    barrier = pltpu.get_barrier_semaphore()
    greeted = [sibling, cross, at(z, y, 1 - xl)]
    greeted += [at(z_peer(d), y, xl) for d in range(1, NZ)]
    greeted += [at(z, y_peer(d), xl) for d in range(1, NY)]
    greeted += [at(z, y_peer(d), 1 - xl) for d in range(1, NY)]
    for device in greeted:
        pl.semaphore_signal(barrier, inc=1, device_id=device, device_id_type=MESH)

    loads[0].wait()
    for c in range(NZ):
        wf[c, rank_rows(f), :] = ms[:, c * CW:(c + 1) * CW].astype(BF16)

    pl.semaphore_wait(barrier, len(greeted))

    for c in range(EARLY):
        w_cross(c, f).start()
    for c in range(NZ):
        w_sib(c, f).start()

    for k in (1, 2, 3):
        loads[k].wait()
    outer_new = OUTER_MOMENTUM * sm[1] + sm[2]
    anchor_new = sm[0] - OUTER_RATE * (sm[2] + OUTER_MOMENTUM * outer_new)
    smo[0] = anchor_new
    smo[1] = outer_new
    mt[y, z, pl.ds(pl.multiple_of(xl * FEAT, FEAT), FEAT), :] = anchor_new.astype(BF16)
    m_x(xl).start()

    loads[4].wait()

    @pl.loop(0, TOK // 16, unroll=2)
    def _(i):
        rows = pl.ds(pl.multiple_of(i * 16, 16), 16)
        x = tk[rows, :].astype(F32)
        inverse = lax.rsqrt(jnp.sum(x * x, axis=-1, keepdims=True) * (1.0 / WIDTH) + EPS_NORM)
        iv[rows, :] = jnp.broadcast_to(inverse, (16, 128))
        scaled = (x * inverse).astype(BF16)
        for c in range(NZ):
            nm[c, rows, :] = scaled[:, c * CW:(c + 1) * CW]

    m_x(1 - xl).wait_recv()
    for d in range(1, NZ):
        m_z(z_peer(d), z).start()

    for k in (5, 6, 7):
        loads[k].wait()

    @pl.loop(0, TOK // 64)
    def _(i):
        rows = pl.ds(pl.multiple_of(i * 64, 64), 64)
        cosine, sine = cs[rows, :], sn[rows, :]
        for b in range(KEYS // 128):
            v = ct[rows, b * 128:(b + 1) * 128].astype(F32)
            kg[rows, b * 128:(b + 1) * 128] = (v * cosine - swap_halves(v) * sine).astype(BF16)

    for k, rank in enumerate((f, f_cross, f_sib, f_diag)):
        kgt[k * ROWS:(k + 1) * ROWS, :] = kg[:, rank_rows(rank)].astype(F32).T.astype(BF16)

    @pl.loop(0, NZ + LAG)
    def _(i):
        @pl.when(i < NZ)
        def _():
            c = chunk(i)
            gb[c] = jnp.dot(kgt[...], nm[c], preferred_element_type=F32).astype(BF16)
            g_sib(c).start()

        @pl.when(i >= LAG)
        def _():
            c = chunk(i - LAG)
            g_sib(c).wait_recv()
            xs[c] = (
                gb[c, ROWS:2 * ROWS, :].astype(F32) + rs[c, ROWS:2 * ROWS, :].astype(F32)
            ).astype(BF16)
            g_cross(c).start()

        @pl.when(lax.rem(i, 3) == 1)
        def _():
            c = lax.div(i, 3)
            w_cross(c, f_cross).wait_recv()
            w_fwd(c, f_cross).start()

    for d in range(1, NZ):
        m_z(z, z_peer(d)).wait_recv()
    for d in range(1, NY):
        m_y(y_peer(d), y).start()

    pj[...] = jnp.zeros_like(pj)
    acc[...] = jnp.zeros_like(acc)

    def use_weights(c):
        w_sib(c, f_sib).wait_recv()
        w_fwd(c, f_diag).wait_recv()

        @pl.loop(0, 2)
        def _(i):
            rows = pl.ds(pl.multiple_of(i * 256, 256), 256)
            w = wf[c]
            pj[rows, :] += lax.dot_general(
                nm[c, rows, :], w, (((1,), (1,)), ((), ())), preferred_element_type=F32
            )
            hidden = jnp.dot(kg[rows, :], w, preferred_element_type=F32)
            hd[c, rows, :] = hidden
            product = hidden * tk[rows, cols(c)].astype(F32)
            acc[rows, :] += product[:, :128] + product[:, 128:]

    for k in (8, 9):
        loads[k].wait()
    steps = jnp.full((8, 128), stp[0], jnp.int32).astype(F32)
    inverse_one = (1.0 / (1.0 - jnp.exp(steps * math.log(BETA_ONE))))[0:1, 0:1]
    inverse_two = (1.0 / (1.0 - jnp.exp(steps * math.log(BETA_TWO))))[0:1, 0:1]

    @pl.loop(0, NZ)
    def _(i):
        c = chunk(i)
        g_cross(c).wait_recv()

        @pl.loop(0, ROWS // 32)
        def _(k):
            rows = pl.ds(pl.multiple_of(k * 32, 32), 32)
            g = (gb[c, rows, :].astype(F32) + rs[c, rows, :].astype(F32)) + xr[c, rows, :].astype(F32)
            one = BETA_ONE * m1[rows, cols(c)] + (1.0 - BETA_ONE) * g
            two = BETA_TWO * m2[rows, cols(c)] + (1.0 - BETA_TWO) * g * g
            m1n[rows, cols(c)] = one
            m2n[rows, cols(c)] = two
            update = (one * inverse_one) / (jnp.sqrt(two * inverse_two) + EPS_ADAM)
            master = ms[rows, cols(c)]
            inner = master - LEARN_RATE * (update + WEIGHT_DECAY * master)
            pv[rows, cols(c)] = inner
            ib[c, rows, :] = inner.astype(BF16)

        @pl.when(i < NZ - 1)
        def _():
            sum_z(c, z).start()

        @pl.when(i >= 5)
        def _():
            w_cross(i - 1, f).start()

        @pl.when(i == 7)
        def _():
            w_cross(7, f).start()

        @pl.when(i < EARLY)
        def _():
            use_weights(i)

    for d in range(1, NY):
        m_y(y, y_peer(d)).wait_recv()

    @pl.loop(0, NZ)
    def _(c):
        merged = mt[:, c].astype(F32).reshape(CW, ROWS).T
        pv[:, cols(c)] = 0.5 * pv[:, cols(c)] + 0.5 * merged

    def forward(c):
        w_cross(c, f_cross).wait_recv()
        w_fwd(c, f_cross).start()

    forward(4)

    total = ib[z].astype(F32)
    for d in range(1, NZ):
        sum_z(z, z_peer(d)).wait_recv()
        total = total + rb[z_peer(d)].astype(F32)
    total = total.T
    qs[...] = total.astype(BF16)
    for d in range(1, 8):
        yy, xx = yx_peer(d)
        sum_yx(yy, xx, y * 2 + xl).start()

    @pl.loop(5, NZ)
    def _(c):
        forward(c)
        use_weights(c - 1)

    own = y * 2 + xl
    total = qs[pl.ds(pl.multiple_of(own * FEAT, FEAT), FEAT), :].astype(F32)
    for d in range(1, 8):
        yy, xx = yx_peer(d)
        sum_yx(y, xl, yy * 2 + xx).wait_recv()
        total = total + qr[yy * 2 + xx].astype(F32)
    smo[2] = sm[0] - total * (1.0 / 64.0)

    use_weights(NZ - 1)

    @pl.loop(0, NZ)
    def _(c):
        w_sib(c, f).wait_send()
        w_cross(c, f).wait_send()
        w_fwd(c, f_cross).wait_send()
        g_sib(c).wait_send()
        g_cross(c).wait_send()

    for d in range(1, NZ):
        sum_z(z_peer(d), z).wait_send()
        m_z(z_peer(d), z).wait_send()
    for d in range(1, 8):
        yy, xx = yx_peer(d)
        sum_yx(yy, xx, y * 2 + xl).wait_send()
    for d in range(1, NY):
        m_y(y_peer(d), y).wait_send()
    m_x(xl).wait_send()

def finish_kernel(
    tk, cs, sn, iv, pj, hd, acc, pv, m1n, m2n, smo,
    key_h, ing_h, par_h, m1n_h, m2n_h, ancn_h, omn_h, penn_h,
    igv, kov, st,
):
    whole = [
        pltpu.make_async_copy(m1n, m1n_h, st.at[0]),
        pltpu.make_async_copy(m2n, m2n_h, st.at[1]),
        pltpu.make_async_copy(pv, par_h, st.at[2]),
        pltpu.make_async_copy(smo.at[0], ancn_h, st.at[3]),
        pltpu.make_async_copy(smo.at[1], omn_h, st.at[4]),
        pltpu.make_async_copy(smo.at[2], penn_h, st.at[5]),
    ]
    for copy in whole:
        copy.start()

    @pl.loop(0, TOK // 128)
    def _(j):
        @pl.loop(0, 4)
        def _(k):
            rows = pl.ds(pl.multiple_of(j * 128 + k * 32, 32), 32)
            inverse = iv[rows, :]
            mean = jnp.sum(acc[rows, :], axis=-1, keepdims=True) * (1.0 / WIDTH)
            coef = inverse * inverse * inverse * mean
            for c in range(NZ):
                for b in range(2):
                    left = c * CW + b * 128
                    igv[rows, left:left + 128] = (
                        inverse * hd[c, rows, b * 128:(b + 1) * 128]
                        - tk[rows, left:left + 128].astype(F32) * coef
                    ).astype(BF16)

        rows = pl.ds(pl.multiple_of(j * 128, 128), 128)
        pltpu.make_async_copy(igv.at[rows], ing_h.at[rows], st.at[6]).start()

    @pl.loop(0, TOK // 64)
    def _(i):
        rows = pl.ds(pl.multiple_of(i * 64, 64), 64)
        cosine, sine = cs[rows, :], sn[rows, :]
        for b in range(KEYS // 128):
            v = pj[rows, b * 128:(b + 1) * 128]
            kov[rows, b * 128:(b + 1) * 128] = (v * cosine + swap_halves(v) * sine).astype(BF16)

    keys_out = pltpu.make_async_copy(kov, key_h, st.at[7])
    keys_out.start()
    for copy in whole:
        copy.wait()
    pltpu.make_async_copy(igv, ing_h, st.at[6]).wait()
    keys_out.wait()


def on_device(
    tokens, cotangent, step_count, master, first_moment, moment_second,
    anchor, outer_moment, pending,
):
    cosine, sine = rope_tables()
    any_spec = pl.BlockSpec(memory_space=pl.ANY)
    vmem_spec = pl.BlockSpec(memory_space=pltpu.VMEM)
    vmem = pltpu.VMEM
    dma = pltpu.SemaphoreType.DMA
    shape = jax.ShapeDtypeStruct
    inputs = (
        tokens, cotangent, master[0], first_moment[0], moment_second[0],
        anchor.T, outer_moment.T, pending.T, jnp.asarray(cosine), jnp.asarray(sine),
    )
    inputs = [pltpu.with_memory_space_constraint(x, pltpu.HBM) for x in inputs]
    held = pl.pallas_call(
        step_kernel,
        out_shape=(
            shape((TOK, WIDTH), BF16),
            shape((TOK, 128), F32),
            shape((TOK, 128), F32),
            shape((TOK, 128), F32),
            shape((TOK, KEYS), F32),
            shape((NZ, TOK, CW), F32),
            shape((TOK, 128), F32),
            shape((ROWS, WIDTH), F32),
            shape((ROWS, WIDTH), F32),
            shape((ROWS, WIDTH), F32),
            shape((3, FEAT, ROWS), F32),
        ),
        in_specs=[pl.BlockSpec(memory_space=pltpu.SMEM)] + [any_spec] * 10,
        out_specs=(vmem_spec,) * 11,
        scratch_shapes=[
            vmem((TOK, KEYS), BF16),
            vmem((ROWS, WIDTH), F32),
            vmem((ROWS, WIDTH), F32),
            vmem((ROWS, WIDTH), F32),
            vmem((3, FEAT, ROWS), F32),
            vmem((NZ, TOK, CW), BF16),
            vmem((TOK, KEYS), BF16),
            vmem((KEYS, TOK), BF16),
            vmem((NZ, KEYS, CW), BF16),
            vmem((NZ, KEYS, CW), BF16),
            vmem((NZ, 2 * ROWS, CW), BF16),
            vmem((NZ, ROWS, CW), BF16),
            vmem((NZ, ROWS, CW), BF16),
            vmem((NZ, ROWS, CW), BF16),
            vmem((NZ, ROWS, CW), BF16),
            vmem((CW, ROWS), BF16),
            vmem((8, FEAT, ROWS), BF16),
            vmem((NY, NZ, 2 * FEAT, ROWS), BF16),
            dma((10,)),
            dma((NZ,)), dma((NZ,)), dma((NZ,)), dma((NZ,)), dma((NZ,)), dma((NZ,)),
            dma((NZ,)), dma((NZ,)), dma((NZ,)), dma((NZ,)),
            dma((NZ,)), dma((NZ,)), dma((8,)), dma((8,)),
            dma((2,)), dma((NZ,)), dma((NZ,)), dma((NY,)), dma((NY,)),
        ],
        compiler_params=pltpu.CompilerParams(
            collective_id=0, has_side_effects=True, vmem_limit_bytes=36 * 2**20
        ),
        name="step",
    )(step_count, *inputs)
    small = shape((FEAT, ROWS), F32)
    state = shape((ROWS, WIDTH), F32)
    outs = pl.pallas_call(
        finish_kernel,
        out_shape=(
            shape((TOK, KEYS), BF16), shape((TOK, WIDTH), BF16),
            state, state, state, small, small, small,
        ),
        in_specs=[vmem_spec] * 11,
        out_specs=(any_spec,) * 8,
        scratch_shapes=[vmem((TOK, WIDTH), BF16), vmem((TOK, KEYS), BF16), dma((8,))],
        compiler_params=pltpu.CompilerParams(vmem_limit_bytes=24 * 2**20),
        name="finish",
    )(*held)
    key_out, input_grad, params, one, two, anchor_new, outer_new, pending_new = outs
    return (
        key_out, input_grad, params[None], one[None], two[None],
        anchor_new.T, outer_new.T, pending_new.T,
    )


def solution(mesh):
    in_specs = (
        P(("replica", "fsdp"), None),
        P(("replica", "fsdp"), None),
        P(),
        P("replica", "fsdp", None),
        P("replica", "fsdp", None),
        P("replica", "fsdp", None),
        P("fsdp", "replica"),
        P("fsdp", "replica"),
        P("fsdp", "replica"),
    )
    out_specs = (
        P(("replica", "fsdp"), None),
        P(("replica", "fsdp"), None),
        P("replica", "fsdp", None),
        P("replica", "fsdp", None),
        P("replica", "fsdp", None),
        P("fsdp", "replica"),
        P("fsdp", "replica"),
        P("fsdp", "replica"),
    )
    return jax.shard_map(
        on_device, mesh=mesh, in_specs=in_specs, out_specs=out_specs, check_vma=False
    )
```

```python
import math

import jax
import jax.numpy as jnp
import numpy as np
from jax import lax
from jax.experimental import pallas as pl
from jax.experimental.pallas import tpu as pltpu
from jax.sharding import PartitionSpec as P

MESH = pl.DeviceIdType.MESH
F32 = jnp.float32
BF16 = jnp.bfloat16

HEAD_DIM = 64
ROPE_BASE = 500000.0
EPS_NORM = 1e-05
BETA_ONE = 0.9
BETA_TWO = 0.95
EPS_ADAM = 1e-08
LEARN_RATE = 0.1
WEIGHT_DECAY = 0.1
OUTER_RATE = 0.7
OUTER_MOMENTUM = 0.9

TOK = 512
WIDTH = 2048
KEYS = 512
ROWS = 128
NZ, NY = 8, 4
CW = WIDTH // NZ
FEAT = 32
EARLY = 4
LAG = 3
LAG_Y = 2


def rope_tables():
    lane = np.arange(128)
    exponent = 2.0 * (lane % HEAD_DIM % (HEAD_DIM // 2)) / HEAD_DIM
    angles = np.arange(TOK)[:, None] * np.exp(-exponent * math.log(ROPE_BASE))[None, :]
    sign = np.where(lane % HEAD_DIM < HEAD_DIM // 2, -1.0, 1.0)[None, :]
    scale = 1.0 / math.sqrt(WIDTH)
    return (
        (np.cos(angles) * scale).astype(np.float32),
        (np.sin(angles) * sign * scale).astype(np.float32),
    )


def swap_halves(values):
    lane = lax.broadcasted_iota(jnp.int32, values.shape, 1)
    first = lax.rem(lane, HEAD_DIM) < HEAD_DIM // 2
    return jnp.where(first, pltpu.roll(values, 96, 1), pltpu.roll(values, 32, 1))


def step_kernel(
    stp, tok_h, cot_h, mas_h, m1_h, m2_h, anc_h, om_h, pen_h, cos_h, sin_h,
    tk, cs, sn, iv, pj, hd, acc, pv, m1n, m2n, smo,
    ct, ms, m1, m2, sm, nm, kg, kgt, wf, gb, rs, xs, xr, ib, yb, zs, zd, zo, qs, qr, mt,
    ld,
    wss, wsr, wxs, wxr, wfs, wfr,
    gss, gsr, gxs, gxr, yss, ysr, zss, zdr, qsem,
    a1, a2s, a2r, a3s, a3r, ready,
):
    r = lax.axis_index("replica")
    f = lax.axis_index("fsdp")
    z = lax.div(r, 8)
    y = lax.rem(lax.div(r, 2), 4)
    xl = lax.rem(r, 2)
    core = lax.rem(f, 2)
    f_sib = f + 1 - 2 * core
    f_cross = lax.rem(f + 2, 4)
    f_diag = lax.rem(f_sib + 2, 4)
    sibling = (r, f_sib)
    cross = (r, f_cross)

    def at(zz, yy, xx):
        return ((zz * NY + yy) * 2 + xx, f)

    def y_peer(d):
        return lax.rem(y + d, NY)

    def rcopy(src, dst, send, recv, device):
        return pltpu.make_async_remote_copy(
            src_ref=src, dst_ref=dst, send_sem=send, recv_sem=recv,
            device_id=device, device_id_type=MESH,
        )

    def rank_rows(rank):
        return pl.ds(pl.multiple_of(rank * ROWS, ROWS), ROWS)

    def cols(c):
        return pl.ds(pl.multiple_of(c * CW, CW), CW)

    def w_sib(c, rank):
        block = wf.at[c, rank_rows(rank)]
        return rcopy(block, block, wss.at[c], wsr.at[c], sibling)

    def w_cross(c, rank):
        block = wf.at[c, rank_rows(rank)]
        return rcopy(block, block, wxs.at[c], wxr.at[c], cross)

    def w_fwd(c, rank):
        block = wf.at[c, rank_rows(rank)]
        return rcopy(block, block, wfs.at[c], wfr.at[c], sibling)

    def g_sib(c):
        return rcopy(
            gb.at[c, pl.ds(2 * ROWS, 2 * ROWS)], rs.at[c], gss.at[c], gsr.at[c], sibling
        )

    def g_cross(c):
        return rcopy(xs.at[c], xr.at[c], gxs.at[c], gxr.at[c], cross)

    def sum_y(c, yy, slot):
        return rcopy(
            ib.at[c, yy], yb.at[c, slot], yss.at[c, yy], ysr.at[c, slot], at(z, yy, xl)
        )

    def sum_z(c, slot):
        return rcopy(zs.at[c], zd.at[slot], zss.at[c], zdr.at[slot], at(c, y, xl))

    def half(part):
        return pl.ds(pl.multiple_of(part * FEAT, FEAT), FEAT)

    def sum_x():
        return rcopy(qs.at[half(1 - xl)], qr, qsem.at[0], qsem.at[1], at(z, y, 1 - xl))

    def m_x(slot):
        block = mt.at[y, z, half(slot)]
        return rcopy(block, block, a1.at[0], a1.at[1], at(z, y, 1 - xl))

    def m_z(zz, slot):
        block = mt.at[y, slot]
        return rcopy(block, block, a2s.at[zz], a2r.at[slot], at(zz, y, xl))

    def m_y(yy, slot):
        block = mt.at[slot]
        return rcopy(block, block, a3s.at[yy], a3r.at[slot], at(z, yy, xl))

    loads = [
        pltpu.make_async_copy(mas_h, ms, ld.at[0]),
        pltpu.make_async_copy(anc_h, sm.at[0], ld.at[1]),
        pltpu.make_async_copy(om_h, sm.at[1], ld.at[2]),
        pltpu.make_async_copy(pen_h, sm.at[2], ld.at[3]),
        pltpu.make_async_copy(tok_h, tk, ld.at[4]),
        pltpu.make_async_copy(cot_h, ct, ld.at[5]),
        pltpu.make_async_copy(cos_h, cs, ld.at[6]),
        pltpu.make_async_copy(sin_h, sn, ld.at[7]),
        pltpu.make_async_copy(m1_h, m1, ld.at[8]),
        pltpu.make_async_copy(m2_h, m2, ld.at[9]),
    ]
    for load in loads[:8]:
        load.start()

    barrier = pltpu.get_barrier_semaphore()

    def greet(device):
        pl.semaphore_signal(barrier, inc=1, device_id=device, device_id_type=MESH)

    greet(sibling)
    greet(cross)
    greet(at(z, y, 1 - xl))
    for d in range(1, NY):
        greet(at(z, y_peer(d), xl))
    for t in range(NZ):
        @pl.when(t > z)
        def _():
            greet(at(t, y, xl))

    loads[0].wait()
    for c in range(NZ):
        wf[c, rank_rows(f), :] = ms[:, c * CW:(c + 1) * CW].astype(BF16)

    for k in (1, 2, 3):
        loads[k].wait()
    outer_new = OUTER_MOMENTUM * sm[1] + sm[2]
    anchor_new = sm[0] - OUTER_RATE * (sm[2] + OUTER_MOMENTUM * outer_new)
    smo[0] = anchor_new
    smo[1] = outer_new
    mt[y, z, half(xl), :] = anchor_new.astype(BF16)

    pl.semaphore_wait(barrier, 6 + z)
    for t in range(NZ):
        @pl.when(t < z)
        def _():
            pl.semaphore_signal(ready, inc=1, device_id=at(t, y, xl), device_id_type=MESH)

    m_x(xl).start()
    for c in range(EARLY):
        w_cross(c, f).start()
    for c in range(NZ):
        w_sib(c, f).start()

    loads[4].wait()
    for load in loads[8:]:
        load.start()

    @pl.loop(0, TOK // 16, unroll=2)
    def _(i):
        rows = pl.ds(pl.multiple_of(i * 16, 16), 16)
        x = tk[rows, :].astype(F32)
        inverse = lax.rsqrt(jnp.sum(x * x, axis=-1, keepdims=True) * (1.0 / WIDTH) + EPS_NORM)
        iv[rows, :] = jnp.broadcast_to(inverse, (16, 128))
        scaled = (x * inverse).astype(BF16)
        for c in range(NZ):
            nm[c, rows, :] = scaled[:, c * CW:(c + 1) * CW]

    m_x(1 - xl).wait_recv()
    for t in range(NZ):
        @pl.when(t < z)
        def _():
            m_z(t, z).start()

    for k in (5, 6, 7):
        loads[k].wait()

    @pl.loop(0, TOK // 64)
    def _(i):
        rows = pl.ds(pl.multiple_of(i * 64, 64), 64)
        cosine, sine = cs[rows, :], sn[rows, :]
        for b in range(KEYS // 128):
            v = ct[rows, b * 128:(b + 1) * 128].astype(F32)
            kg[rows, b * 128:(b + 1) * 128] = (v * cosine - swap_halves(v) * sine).astype(BF16)

    for k, rank in enumerate((f, f_cross, f_sib, f_diag)):
        kgt[k * ROWS:(k + 1) * ROWS, :] = kg[:, rank_rows(rank)].astype(F32).T.astype(BF16)

    @pl.loop(0, NZ + LAG)
    def _(i):
        @pl.when(i < NZ)
        def _():
            c = i
            gb[c] = jnp.dot(kgt[...], nm[c], preferred_element_type=F32).astype(BF16)
            g_sib(c).start()

        @pl.when(i >= LAG)
        def _():
            c = i - LAG
            g_sib(c).wait_recv()
            xs[c] = (
                gb[c, ROWS:2 * ROWS, :].astype(F32) + rs[c, ROWS:2 * ROWS, :].astype(F32)
            ).astype(BF16)
            g_cross(c).start()

        @pl.when((lax.rem(i, 3) == 1) & (i < 3 * EARLY))
        def _():
            c = lax.div(i, 3)
            w_cross(c, f_cross).wait_recv()
            w_fwd(c, f_cross).start()

    @pl.when(z < NZ - 1)
    def _():
        pl.semaphore_wait(ready, NZ - 1 - z)

    for t in range(NZ):
        @pl.when(t > z)
        def _():
            m_z(t, z).start()

    pj[...] = jnp.zeros_like(pj)
    acc[...] = jnp.zeros_like(acc)

    def use_weights(c):
        w_sib(c, f_sib).wait_recv()
        w_fwd(c, f_diag).wait_recv()

        @pl.loop(0, 2)
        def _(i):
            rows = pl.ds(pl.multiple_of(i * 256, 256), 256)
            w = wf[c]
            pj[rows, :] += lax.dot_general(
                nm[c, rows, :], w, (((1,), (1,)), ((), ())), preferred_element_type=F32
            )
            hidden = jnp.dot(kg[rows, :], w, preferred_element_type=F32)
            hd[c, rows, :] = hidden
            product = hidden * tk[rows, cols(c)].astype(F32)
            acc[rows, :] += product[:, :128] + product[:, 128:]

    for k in (8, 9):
        loads[k].wait()
    steps = jnp.full((8, 128), stp[0], jnp.int32).astype(F32)
    inverse_one = (1.0 / (1.0 - jnp.exp(steps * math.log(BETA_ONE))))[0:1, 0:1]
    inverse_two = (1.0 / (1.0 - jnp.exp(steps * math.log(BETA_TWO))))[0:1, 0:1]

    def forward(c):
        w_cross(c, f_cross).wait_recv()
        w_fwd(c, f_cross).start()

    def adam(c):
        g_cross(c).wait_recv()

        @pl.loop(0, ROWS // 32)
        def _(k):
            rows = pl.ds(pl.multiple_of(k * 32, 32), 32)
            g = (gb[c, rows, :].astype(F32) + rs[c, rows, :].astype(F32)) + xr[c, rows, :].astype(F32)
            one = BETA_ONE * m1[rows, cols(c)] + (1.0 - BETA_ONE) * g
            two = BETA_TWO * m2[rows, cols(c)] + (1.0 - BETA_TWO) * g * g
            m1n[rows, cols(c)] = one
            m2n[rows, cols(c)] = two
            update = (one * inverse_one) / (jnp.sqrt(two * inverse_two) + EPS_ADAM)
            master = ms[rows, cols(c)]
            inner = master - LEARN_RATE * (update + WEIGHT_DECAY * master)
            pv[rows, cols(c)] = inner

        turned = pv[:, cols(c)].T.astype(BF16)
        for k in range(NY):
            ib[c, k] = turned[k * 2 * FEAT:(k + 1) * 2 * FEAT]
        for d in range(1, NY):
            sum_y(c, y_peer(d), y).start()

    def pass_on(c):
        total = ib[c, y].astype(F32)
        for d in range(1, NY):
            sum_y(c, y, y_peer(d)).wait_recv()
            total = total + yb[c, y_peer(d)].astype(F32)
        zs[c] = total.astype(BF16)

        @pl.when(c == z)
        def _():
            zo[...] = total

        @pl.when(c != z)
        def _():
            sum_z(c, z).start()

    def sum_last():
        for t in range(NZ):
            @pl.when(t != z)
            def _():
                sum_z(z, t).wait_recv()
                zo[...] += zd[t].astype(F32)
        qs[...] = zo[...]
        sum_x().start()

    @pl.loop(0, 2 * NZ - EARLY)
    def _(i):
        @pl.when(i < NZ)
        def _():
            adam(i)

        for k in range(3):
            @pl.when(i == NZ - 3 + k)
            def _():
                for c in range(EARLY + k, NZ, 3):
                    w_cross(c, f).start()

        @pl.when(i == NZ - 1)
        def _():
            for t in range(NZ):
                @pl.when(t != z)
                def _():
                    m_z(z, t).wait_recv()
            for d in range(1, NY):
                m_y(y_peer(d), y).start()

        @pl.when(i >= NZ)
        def _():
            forward(i - NZ + EARLY)

        @pl.when(i < EARLY)
        def _():
            use_weights(i)

        @pl.when(i > NZ)
        def _():
            use_weights(i - NZ + EARLY - 1)

        @pl.when((i >= LAG_Y) & (i < NZ + LAG_Y))
        def _():
            pass_on(i - LAG_Y)

    sum_last()

    for d in range(1, NY):
        m_y(y, y_peer(d)).wait_recv()

    @pl.loop(0, NZ)
    def _(c):
        merged = mt[:, c].astype(F32).reshape(CW, ROWS).T
        pv[:, cols(c)] = 0.5 * pv[:, cols(c)] + 0.5 * merged

    use_weights(NZ - 1)

    sum_x().wait_recv()
    smo[2] = sm[0] - (qs[half(xl), :] + qr[...]) * (1.0 / 64.0)

    @pl.loop(0, NZ)
    def _(c):
        w_sib(c, f).wait_send()
        w_cross(c, f).wait_send()
        w_fwd(c, f_cross).wait_send()
        g_sib(c).wait_send()
        g_cross(c).wait_send()

    for c in range(NZ):
        for d in range(1, NY):
            sum_y(c, y_peer(d), y).wait_send()

        @pl.when(c != z)
        def _():
            sum_z(c, z).wait_send()
            m_z(c, z).wait_send()
    sum_x().wait_send()
    for d in range(1, NY):
        m_y(y_peer(d), y).wait_send()
    m_x(xl).wait_send()

def finish_kernel(
    tk, cs, sn, iv, pj, hd, acc, pv, m1n, m2n, smo,
    key_h, ing_h, par_h, m1n_h, m2n_h, ancn_h, omn_h, penn_h,
    igv, kov, co, st,
):
    whole = [
        pltpu.make_async_copy(m1n, m1n_h, st.at[0]),
        pltpu.make_async_copy(m2n, m2n_h, st.at[1]),
        pltpu.make_async_copy(pv, par_h, st.at[2]),
        pltpu.make_async_copy(smo.at[0], ancn_h, st.at[3]),
        pltpu.make_async_copy(smo.at[1], omn_h, st.at[4]),
        pltpu.make_async_copy(smo.at[2], penn_h, st.at[5]),
    ]
    for copy in whole:
        copy.start()

    mean = jnp.sum(acc[...], axis=-1, keepdims=True) * (1.0 / WIDTH)
    co[...] = iv[...] * iv[...] * iv[...] * mean

    @pl.loop(0, TOK // 128)
    def _(j):
        @pl.loop(0, 4)
        def _(k):
            rows = pl.ds(pl.multiple_of(j * 128 + k * 32, 32), 32)
            inverse = iv[rows, :]
            coef = co[rows, :]
            for c in range(NZ):
                for b in range(2):
                    left = c * CW + b * 128
                    igv[rows, left:left + 128] = (
                        inverse * hd[c, rows, b * 128:(b + 1) * 128]
                        - tk[rows, left:left + 128].astype(F32) * coef
                    ).astype(BF16)

        rows = pl.ds(pl.multiple_of(j * 128, 128), 128)
        pltpu.make_async_copy(igv.at[rows], ing_h.at[rows], st.at[6]).start()

    @pl.loop(0, TOK // 64)
    def _(i):
        rows = pl.ds(pl.multiple_of(i * 64, 64), 64)
        cosine, sine = cs[rows, :], sn[rows, :]
        for b in range(KEYS // 128):
            v = pj[rows, b * 128:(b + 1) * 128]
            kov[rows, b * 128:(b + 1) * 128] = (v * cosine + swap_halves(v) * sine).astype(BF16)

    keys_out = pltpu.make_async_copy(kov, key_h, st.at[7])
    keys_out.start()
    for copy in whole:
        copy.wait()
    pltpu.make_async_copy(igv, ing_h, st.at[6]).wait()
    keys_out.wait()


def on_device(
    tokens, cotangent, step_count, master, first_moment, moment_second,
    anchor, outer_moment, pending,
):
    cosine, sine = rope_tables()
    any_spec = pl.BlockSpec(memory_space=pl.ANY)
    vmem_spec = pl.BlockSpec(memory_space=pltpu.VMEM)
    vmem = pltpu.VMEM
    dma = pltpu.SemaphoreType.DMA
    shape = jax.ShapeDtypeStruct
    inputs = (
        tokens, cotangent, master[0], first_moment[0], moment_second[0],
        anchor.T, outer_moment.T, pending.T, jnp.asarray(cosine), jnp.asarray(sine),
    )
    inputs = [pltpu.with_memory_space_constraint(x, pltpu.HBM) for x in inputs]
    held = pl.pallas_call(
        step_kernel,
        out_shape=(
            shape((TOK, WIDTH), BF16),
            shape((TOK, 128), F32),
            shape((TOK, 128), F32),
            shape((TOK, 128), F32),
            shape((TOK, KEYS), F32),
            shape((NZ, TOK, CW), F32),
            shape((TOK, 128), F32),
            shape((ROWS, WIDTH), F32),
            shape((ROWS, WIDTH), F32),
            shape((ROWS, WIDTH), F32),
            shape((3, FEAT, ROWS), F32),
        ),
        in_specs=[pl.BlockSpec(memory_space=pltpu.SMEM)] + [any_spec] * 10,
        out_specs=(vmem_spec,) * 11,
        scratch_shapes=[
            vmem((TOK, KEYS), BF16),
            vmem((ROWS, WIDTH), F32),
            vmem((ROWS, WIDTH), F32),
            vmem((ROWS, WIDTH), F32),
            vmem((3, FEAT, ROWS), F32),
            vmem((NZ, TOK, CW), BF16),
            vmem((TOK, KEYS), BF16),
            vmem((KEYS, TOK), BF16),
            vmem((NZ, KEYS, CW), BF16),
            vmem((NZ, KEYS, CW), BF16),
            vmem((NZ, 2 * ROWS, CW), BF16),
            vmem((NZ, ROWS, CW), BF16),
            vmem((NZ, ROWS, CW), BF16),
            vmem((NZ, NY, 2 * FEAT, ROWS), BF16),
            vmem((NZ, NY, 2 * FEAT, ROWS), BF16),
            vmem((NZ, 2 * FEAT, ROWS), BF16),
            vmem((NZ, 2 * FEAT, ROWS), BF16),
            vmem((2 * FEAT, ROWS), F32),
            vmem((2 * FEAT, ROWS), F32),
            vmem((FEAT, ROWS), F32),
            vmem((NY, NZ, 2 * FEAT, ROWS), BF16),
            dma((10,)),
            dma((NZ,)), dma((NZ,)), dma((NZ,)), dma((NZ,)), dma((NZ,)), dma((NZ,)),
            dma((NZ,)), dma((NZ,)), dma((NZ,)), dma((NZ,)),
            dma((NZ, NY)), dma((NZ, NY)), dma((NZ,)), dma((NZ,)), dma((2,)),
            dma((2,)), dma((NZ,)), dma((NZ,)), dma((NY,)), dma((NY,)),
            pltpu.SemaphoreType.REGULAR,
        ],
        compiler_params=pltpu.CompilerParams(
            collective_id=0, has_side_effects=True, vmem_limit_bytes=36 * 2**20
        ),
        name="step",
    )(step_count, *inputs)
    small = shape((FEAT, ROWS), F32)
    state = shape((ROWS, WIDTH), F32)
    outs = pl.pallas_call(
        finish_kernel,
        out_shape=(
            shape((TOK, KEYS), BF16), shape((TOK, WIDTH), BF16),
            state, state, state, small, small, small,
        ),
        in_specs=[vmem_spec] * 11,
        out_specs=(any_spec,) * 8,
        scratch_shapes=[
            vmem((TOK, WIDTH), BF16), vmem((TOK, KEYS), BF16), vmem((TOK, 128), F32), dma((8,)),
        ],
        compiler_params=pltpu.CompilerParams(vmem_limit_bytes=24 * 2**20),
        name="finish",
    )(*held)
    key_out, input_grad, params, one, two, anchor_new, outer_new, pending_new = outs
    return (
        key_out, input_grad, params[None], one[None], two[None],
        anchor_new.T, outer_new.T, pending_new.T,
    )


def solution(mesh):
    in_specs = (
        P(("replica", "fsdp"), None),
        P(("replica", "fsdp"), None),
        P(),
        P("replica", "fsdp", None),
        P("replica", "fsdp", None),
        P("replica", "fsdp", None),
        P("fsdp", "replica"),
        P("fsdp", "replica"),
        P("fsdp", "replica"),
    )
    out_specs = (
        P(("replica", "fsdp"), None),
        P(("replica", "fsdp"), None),
        P("replica", "fsdp", None),
        P("replica", "fsdp", None),
        P("replica", "fsdp", None),
        P("fsdp", "replica"),
        P("fsdp", "replica"),
        P("fsdp", "replica"),
    )
    return jax.shard_map(
        on_device, mesh=mesh, in_specs=in_specs, out_specs=out_specs, check_vma=False
    )
```

```python
import math

import jax
import jax.numpy as jnp
import numpy as np
from jax import lax
from jax.experimental import pallas as pl
from jax.experimental.pallas import tpu as pltpu
from jax.sharding import PartitionSpec as P

MESH = pl.DeviceIdType.MESH
F32 = jnp.float32
BF16 = jnp.bfloat16

HEAD_DIM = 64
ROPE_BASE = 500000.0
EPS_NORM = 1e-05
BETA_ONE = 0.9
BETA_TWO = 0.95
EPS_ADAM = 1e-08
LEARN_RATE = 0.1
WEIGHT_DECAY = 0.1
OUTER_RATE = 0.7
OUTER_MOMENTUM = 0.9

TOK = 512
WIDTH = 2048
KEYS = 512
ROWS = 128
NZ, NY = 8, 4
CW = WIDTH // NZ
FEAT = 32
EARLY = 4
LAG = 3
LAG_Y = 2


def rope_tables():
    lane = np.arange(128)
    exponent = 2.0 * (lane % HEAD_DIM % (HEAD_DIM // 2)) / HEAD_DIM
    angles = np.arange(TOK)[:, None] * np.exp(-exponent * math.log(ROPE_BASE))[None, :]
    sign = np.where(lane % HEAD_DIM < HEAD_DIM // 2, -1.0, 1.0)[None, :]
    scale = 1.0 / math.sqrt(WIDTH)
    return (
        (np.cos(angles) * scale).astype(np.float32),
        (np.sin(angles) * sign * scale).astype(np.float32),
    )


def swap_halves(values):
    lane = lax.broadcasted_iota(jnp.int32, values.shape, 1)
    first = lax.rem(lane, HEAD_DIM) < HEAD_DIM // 2
    return jnp.where(first, pltpu.roll(values, 96, 1), pltpu.roll(values, 32, 1))


def step_kernel(
    stp, tok_h, cot_h, mas_h, m1_h, m2_h, anc_h, om_h, pen_h, cos_h, sin_h,
    tk, cs, sn, iv, pj, hd, acc, pv, m1n, m2n, smo,
    ct, ms, m1, m2, sm, nm, kg, kgt, wf, gb, rs, xs, xr, ib, yb, zs, zd, zo, qs, qr, mt,
    ld,
    wss, wsr, wxs, wxr, wfs, wfr,
    gss, gsr, gxs, gxr, yss, ysr, zss, zdr, qsem,
    a1, a2s, a2r, a3s, a3r, ready,
):
    r = lax.axis_index("replica")
    f = lax.axis_index("fsdp")
    z = lax.div(r, 8)
    y = lax.rem(lax.div(r, 2), 4)
    xl = lax.rem(r, 2)
    core = lax.rem(f, 2)
    f_sib = f + 1 - 2 * core
    f_cross = lax.rem(f + 2, 4)
    f_diag = lax.rem(f_sib + 2, 4)
    sibling = (r, f_sib)
    cross = (r, f_cross)

    def at(zz, yy, xx):
        return ((zz * NY + yy) * 2 + xx, f)

    def y_peer(d):
        return lax.rem(y + d, NY)

    def rcopy(src, dst, send, recv, device):
        return pltpu.make_async_remote_copy(
            src_ref=src, dst_ref=dst, send_sem=send, recv_sem=recv,
            device_id=device, device_id_type=MESH,
        )

    def rank_rows(rank):
        return pl.ds(pl.multiple_of(rank * ROWS, ROWS), ROWS)

    def cols(c):
        return pl.ds(pl.multiple_of(c * CW, CW), CW)

    def w_sib(c, rank):
        block = wf.at[c, rank_rows(rank)]
        return rcopy(block, block, wss.at[c], wsr.at[c], sibling)

    def w_cross(c, rank):
        block = wf.at[c, rank_rows(rank)]
        return rcopy(block, block, wxs.at[c], wxr.at[c], cross)

    def w_fwd(c, rank):
        block = wf.at[c, rank_rows(rank)]
        return rcopy(block, block, wfs.at[c], wfr.at[c], sibling)

    def g_sib(c):
        return rcopy(
            gb.at[c, pl.ds(2 * ROWS, 2 * ROWS)], rs.at[c], gss.at[c], gsr.at[c], sibling
        )

    def g_cross(c):
        return rcopy(xs.at[c], xr.at[c], gxs.at[c], gxr.at[c], cross)

    def sum_y(c, yy, slot):
        return rcopy(
            ib.at[c, yy], yb.at[c, slot], yss.at[c, yy], ysr.at[c, slot], at(z, yy, xl)
        )

    def sum_z(c, slot):
        return rcopy(zs.at[c], zd.at[slot], zss.at[c], zdr.at[slot], at(c, y, xl))

    def half(part):
        return pl.ds(pl.multiple_of(part * FEAT, FEAT), FEAT)

    def sum_x():
        return rcopy(qs.at[half(1 - xl)], qr, qsem.at[0], qsem.at[1], at(z, y, 1 - xl))

    def m_x(slot):
        block = mt.at[y, z, half(slot)]
        return rcopy(block, block, a1.at[0], a1.at[1], at(z, y, 1 - xl))

    def m_z(zz, slot):
        block = mt.at[y, slot]
        return rcopy(block, block, a2s.at[zz], a2r.at[slot], at(zz, y, xl))

    def m_y(yy, slot):
        block = mt.at[slot]
        return rcopy(block, block, a3s.at[yy], a3r.at[slot], at(z, yy, xl))

    loads = [
        pltpu.make_async_copy(mas_h, ms, ld.at[0]),
        pltpu.make_async_copy(anc_h, sm.at[0], ld.at[1]),
        pltpu.make_async_copy(om_h, sm.at[1], ld.at[2]),
        pltpu.make_async_copy(pen_h, sm.at[2], ld.at[3]),
        pltpu.make_async_copy(tok_h, tk, ld.at[4]),
        pltpu.make_async_copy(cot_h, ct, ld.at[5]),
        pltpu.make_async_copy(cos_h, cs, ld.at[6]),
        pltpu.make_async_copy(sin_h, sn, ld.at[7]),
        pltpu.make_async_copy(m1_h, m1, ld.at[8]),
        pltpu.make_async_copy(m2_h, m2, ld.at[9]),
    ]
    for load in loads[:8]:
        load.start()

    barrier = pltpu.get_barrier_semaphore()

    def greet(device):
        pl.semaphore_signal(barrier, inc=1, device_id=device, device_id_type=MESH)

    greet(sibling)
    greet(cross)
    greet(at(z, y, 1 - xl))
    for d in range(1, NY):
        greet(at(z, y_peer(d), xl))
    for t in range(NZ):
        @pl.when(t > z)
        def _():
            greet(at(t, y, xl))

    loads[0].wait()
    for c in range(NZ):
        wf[c, rank_rows(f), :] = ms[:, c * CW:(c + 1) * CW].astype(BF16)

    for k in (1, 2, 3):
        loads[k].wait()
    outer_new = OUTER_MOMENTUM * sm[1] + sm[2]
    anchor_new = sm[0] - OUTER_RATE * (sm[2] + OUTER_MOMENTUM * outer_new)
    smo[0] = anchor_new
    smo[1] = outer_new
    mt[y, z, half(xl), :] = anchor_new.astype(BF16)

    pl.semaphore_wait(barrier, 6 + z)
    for t in range(NZ):
        @pl.when(t < z)
        def _():
            pl.semaphore_signal(ready, inc=1, device_id=at(t, y, xl), device_id_type=MESH)

    m_x(xl).start()
    for c in range(EARLY):
        w_cross(c, f).start()
    for c in range(NZ):
        w_sib(c, f).start()

    loads[4].wait()
    for load in loads[8:]:
        load.start()

    @pl.loop(0, TOK // 16, unroll=2)
    def _(i):
        rows = pl.ds(pl.multiple_of(i * 16, 16), 16)
        x = tk[rows, :].astype(F32)
        inverse = lax.rsqrt(jnp.sum(x * x, axis=-1, keepdims=True) * (1.0 / WIDTH) + EPS_NORM)
        iv[rows, :] = jnp.broadcast_to(inverse, (16, 128))
        scaled = (x * inverse).astype(BF16)
        for c in range(NZ):
            nm[c, rows, :] = scaled[:, c * CW:(c + 1) * CW]

    m_x(1 - xl).wait_recv()
    for t in range(NZ):
        @pl.when(t < z)
        def _():
            m_z(t, z).start()

    for k in (5, 6, 7):
        loads[k].wait()

    @pl.loop(0, TOK // 64)
    def _(i):
        rows = pl.ds(pl.multiple_of(i * 64, 64), 64)
        cosine, sine = cs[rows, :], sn[rows, :]
        for b in range(KEYS // 128):
            v = ct[rows, b * 128:(b + 1) * 128].astype(F32)
            kg[rows, b * 128:(b + 1) * 128] = (v * cosine - swap_halves(v) * sine).astype(BF16)

    for k, rank in enumerate((f, f_cross, f_sib, f_diag)):
        kgt[k * ROWS:(k + 1) * ROWS, :] = kg[:, rank_rows(rank)].astype(F32).T.astype(BF16)

    @pl.loop(0, NZ + LAG)
    def _(i):
        @pl.when(i < NZ)
        def _():
            c = i
            gb[c] = jnp.dot(kgt[...], nm[c], preferred_element_type=F32).astype(BF16)
            g_sib(c).start()

        @pl.when(i >= LAG)
        def _():
            c = i - LAG
            g_sib(c).wait_recv()
            xs[c] = (
                gb[c, ROWS:2 * ROWS, :].astype(F32) + rs[c, ROWS:2 * ROWS, :].astype(F32)
            ).astype(BF16)
            g_cross(c).start()

        @pl.when((lax.rem(i, 3) == 1) & (i < 3 * EARLY))
        def _():
            c = lax.div(i, 3)
            w_cross(c, f_cross).wait_recv()
            w_fwd(c, f_cross).start()

    @pl.when(z < NZ - 1)
    def _():
        pl.semaphore_wait(ready, NZ - 1 - z)

    for t in range(NZ):
        @pl.when(t > z)
        def _():
            m_z(t, z).start()

    pj[...] = jnp.zeros_like(pj)
    acc[...] = jnp.zeros_like(acc)

    def use_weights(c):
        w_sib(c, f_sib).wait_recv()
        w_fwd(c, f_diag).wait_recv()

        @pl.loop(0, 2)
        def _(i):
            rows = pl.ds(pl.multiple_of(i * 256, 256), 256)
            w = wf[c]
            pj[rows, :] += lax.dot_general(
                nm[c, rows, :], w, (((1,), (1,)), ((), ())), preferred_element_type=F32
            )
            hidden = jnp.dot(kg[rows, :], w, preferred_element_type=F32)
            hd[c, rows, :] = hidden
            product = hidden * tk[rows, cols(c)].astype(F32)
            acc[rows, :] += product[:, :128] + product[:, 128:]

    for k in (8, 9):
        loads[k].wait()
    steps = jnp.full((8, 128), stp[0], jnp.int32).astype(F32)
    inverse_one = (1.0 / (1.0 - jnp.exp(steps * math.log(BETA_ONE))))[0:1, 0:1]
    inverse_two = (1.0 / (1.0 - jnp.exp(steps * math.log(BETA_TWO))))[0:1, 0:1]

    def forward(c):
        w_cross(c, f_cross).wait_recv()
        w_fwd(c, f_cross).start()

    def adam(c):
        g_cross(c).wait_recv()

        @pl.loop(0, ROWS // 32)
        def _(k):
            rows = pl.ds(pl.multiple_of(k * 32, 32), 32)
            g = (gb[c, rows, :].astype(F32) + rs[c, rows, :].astype(F32)) + xr[c, rows, :].astype(F32)
            one = BETA_ONE * m1[rows, cols(c)] + (1.0 - BETA_ONE) * g
            two = BETA_TWO * m2[rows, cols(c)] + (1.0 - BETA_TWO) * g * g
            m1n[rows, cols(c)] = one
            m2n[rows, cols(c)] = two
            update = (one * inverse_one) / (jnp.sqrt(two * inverse_two) + EPS_ADAM)
            master = ms[rows, cols(c)]
            inner = master - LEARN_RATE * (update + WEIGHT_DECAY * master)
            pv[rows, cols(c)] = inner

        turned = pv[:, cols(c)].T.astype(BF16)
        for k in range(NY):
            ib[c, k] = turned[k * 2 * FEAT:(k + 1) * 2 * FEAT]
        for d in range(1, NY):
            sum_y(c, y_peer(d), y).start()

    def pass_on(c):
        total = ib[c, y].astype(F32)
        for d in range(1, NY):
            sum_y(c, y, y_peer(d)).wait_recv()
            total = total + yb[c, y_peer(d)].astype(F32)
        zs[c] = total.astype(BF16)

        @pl.when(c == z)
        def _():
            zo[...] = total

        @pl.when(c != z)
        def _():
            sum_z(c, z).start()

    def sum_last():
        for t in range(NZ):
            @pl.when(t != z)
            def _():
                sum_z(z, t).wait_recv()
                zo[...] += zd[t].astype(F32)
        qs[...] = zo[...]
        sum_x().start()

    @pl.loop(0, 2 * NZ - EARLY)
    def _(i):
        @pl.when(i < NZ)
        def _():
            adam(i)

        for k in range(3):
            @pl.when(i == NZ - 5 + k)
            def _():
                for c in range(EARLY + k, NZ, 3):
                    w_cross(c, f).start()

        @pl.when(i == NZ - 1)
        def _():
            for t in range(NZ):
                @pl.when(t != z)
                def _():
                    m_z(z, t).wait_recv()
            for d in range(1, NY):
                m_y(y_peer(d), y).start()

        @pl.when(i >= NZ)
        def _():
            forward(i - NZ + EARLY)

        @pl.when(i < EARLY)
        def _():
            use_weights(i)

        @pl.when(i > NZ)
        def _():
            use_weights(i - NZ + EARLY - 1)

        @pl.when((i >= LAG_Y) & (i < NZ + LAG_Y))
        def _():
            pass_on(i - LAG_Y)

    sum_last()

    for d in range(1, NY):
        m_y(y, y_peer(d)).wait_recv()

    @pl.loop(0, NZ)
    def _(c):
        merged = mt[:, c].astype(F32).reshape(CW, ROWS).T
        pv[:, cols(c)] = 0.5 * pv[:, cols(c)] + 0.5 * merged

    use_weights(NZ - 1)

    sum_x().wait_recv()
    smo[2] = sm[0] - (qs[half(xl), :] + qr[...]) * (1.0 / 64.0)

    @pl.loop(0, NZ)
    def _(c):
        w_sib(c, f).wait_send()
        w_cross(c, f).wait_send()
        w_fwd(c, f_cross).wait_send()
        g_sib(c).wait_send()
        g_cross(c).wait_send()

    for c in range(NZ):
        for d in range(1, NY):
            sum_y(c, y_peer(d), y).wait_send()

        @pl.when(c != z)
        def _():
            sum_z(c, z).wait_send()
            m_z(c, z).wait_send()
    sum_x().wait_send()
    for d in range(1, NY):
        m_y(y_peer(d), y).wait_send()
    m_x(xl).wait_send()

def finish_kernel(
    tk, cs, sn, iv, pj, hd, acc, pv, m1n, m2n, smo,
    key_h, ing_h, par_h, m1n_h, m2n_h, ancn_h, omn_h, penn_h,
    igv, kov, co, st,
):
    whole = [
        pltpu.make_async_copy(m1n, m1n_h, st.at[0]),
        pltpu.make_async_copy(m2n, m2n_h, st.at[1]),
        pltpu.make_async_copy(pv, par_h, st.at[2]),
        pltpu.make_async_copy(smo.at[0], ancn_h, st.at[3]),
        pltpu.make_async_copy(smo.at[1], omn_h, st.at[4]),
        pltpu.make_async_copy(smo.at[2], penn_h, st.at[5]),
    ]
    for copy in whole:
        copy.start()

    mean = jnp.sum(acc[...], axis=-1, keepdims=True) * (1.0 / WIDTH)
    co[...] = iv[...] * iv[...] * iv[...] * mean

    @pl.loop(0, TOK // 128)
    def _(j):
        @pl.loop(0, 4)
        def _(k):
            rows = pl.ds(pl.multiple_of(j * 128 + k * 32, 32), 32)
            inverse = iv[rows, :]
            coef = co[rows, :]
            for c in range(NZ):
                for b in range(2):
                    left = c * CW + b * 128
                    igv[rows, left:left + 128] = (
                        inverse * hd[c, rows, b * 128:(b + 1) * 128]
                        - tk[rows, left:left + 128].astype(F32) * coef
                    ).astype(BF16)

        rows = pl.ds(pl.multiple_of(j * 128, 128), 128)
        pltpu.make_async_copy(igv.at[rows], ing_h.at[rows], st.at[6]).start()

    @pl.loop(0, TOK // 64)
    def _(i):
        rows = pl.ds(pl.multiple_of(i * 64, 64), 64)
        cosine, sine = cs[rows, :], sn[rows, :]
        for b in range(KEYS // 128):
            v = pj[rows, b * 128:(b + 1) * 128]
            kov[rows, b * 128:(b + 1) * 128] = (v * cosine + swap_halves(v) * sine).astype(BF16)

    keys_out = pltpu.make_async_copy(kov, key_h, st.at[7])
    keys_out.start()
    for copy in whole:
        copy.wait()
    pltpu.make_async_copy(igv, ing_h, st.at[6]).wait()
    keys_out.wait()


def on_device(
    tokens, cotangent, step_count, master, first_moment, moment_second,
    anchor, outer_moment, pending,
):
    cosine, sine = rope_tables()
    any_spec = pl.BlockSpec(memory_space=pl.ANY)
    vmem_spec = pl.BlockSpec(memory_space=pltpu.VMEM)
    vmem = pltpu.VMEM
    dma = pltpu.SemaphoreType.DMA
    shape = jax.ShapeDtypeStruct
    inputs = (
        tokens, cotangent, master[0], first_moment[0], moment_second[0],
        anchor.T, outer_moment.T, pending.T, jnp.asarray(cosine), jnp.asarray(sine),
    )
    inputs = [pltpu.with_memory_space_constraint(x, pltpu.HBM) for x in inputs]
    held = pl.pallas_call(
        step_kernel,
        out_shape=(
            shape((TOK, WIDTH), BF16),
            shape((TOK, 128), F32),
            shape((TOK, 128), F32),
            shape((TOK, 128), F32),
            shape((TOK, KEYS), F32),
            shape((NZ, TOK, CW), F32),
            shape((TOK, 128), F32),
            shape((ROWS, WIDTH), F32),
            shape((ROWS, WIDTH), F32),
            shape((ROWS, WIDTH), F32),
            shape((3, FEAT, ROWS), F32),
        ),
        in_specs=[pl.BlockSpec(memory_space=pltpu.SMEM)] + [any_spec] * 10,
        out_specs=(vmem_spec,) * 11,
        scratch_shapes=[
            vmem((TOK, KEYS), BF16),
            vmem((ROWS, WIDTH), F32),
            vmem((ROWS, WIDTH), F32),
            vmem((ROWS, WIDTH), F32),
            vmem((3, FEAT, ROWS), F32),
            vmem((NZ, TOK, CW), BF16),
            vmem((TOK, KEYS), BF16),
            vmem((KEYS, TOK), BF16),
            vmem((NZ, KEYS, CW), BF16),
            vmem((NZ, KEYS, CW), BF16),
            vmem((NZ, 2 * ROWS, CW), BF16),
            vmem((NZ, ROWS, CW), BF16),
            vmem((NZ, ROWS, CW), BF16),
            vmem((NZ, NY, 2 * FEAT, ROWS), BF16),
            vmem((NZ, NY, 2 * FEAT, ROWS), BF16),
            vmem((NZ, 2 * FEAT, ROWS), BF16),
            vmem((NZ, 2 * FEAT, ROWS), BF16),
            vmem((2 * FEAT, ROWS), F32),
            vmem((2 * FEAT, ROWS), F32),
            vmem((FEAT, ROWS), F32),
            vmem((NY, NZ, 2 * FEAT, ROWS), BF16),
            dma((10,)),
            dma((NZ,)), dma((NZ,)), dma((NZ,)), dma((NZ,)), dma((NZ,)), dma((NZ,)),
            dma((NZ,)), dma((NZ,)), dma((NZ,)), dma((NZ,)),
            dma((NZ, NY)), dma((NZ, NY)), dma((NZ,)), dma((NZ,)), dma((2,)),
            dma((2,)), dma((NZ,)), dma((NZ,)), dma((NY,)), dma((NY,)),
            pltpu.SemaphoreType.REGULAR,
        ],
        compiler_params=pltpu.CompilerParams(
            collective_id=0, has_side_effects=True, vmem_limit_bytes=36 * 2**20
        ),
        name="step",
    )(step_count, *inputs)
    small = shape((FEAT, ROWS), F32)
    state = shape((ROWS, WIDTH), F32)
    outs = pl.pallas_call(
        finish_kernel,
        out_shape=(
            shape((TOK, KEYS), BF16), shape((TOK, WIDTH), BF16),
            state, state, state, small, small, small,
        ),
        in_specs=[vmem_spec] * 11,
        out_specs=(any_spec,) * 8,
        scratch_shapes=[
            vmem((TOK, WIDTH), BF16), vmem((TOK, KEYS), BF16), vmem((TOK, 128), F32), dma((8,)),
        ],
        compiler_params=pltpu.CompilerParams(vmem_limit_bytes=24 * 2**20),
        name="finish",
    )(*held)
    key_out, input_grad, params, one, two, anchor_new, outer_new, pending_new = outs
    return (
        key_out, input_grad, params[None], one[None], two[None],
        anchor_new.T, outer_new.T, pending_new.T,
    )


def solution(mesh):
    in_specs = (
        P(("replica", "fsdp"), None),
        P(("replica", "fsdp"), None),
        P(),
        P("replica", "fsdp", None),
        P("replica", "fsdp", None),
        P("replica", "fsdp", None),
        P("fsdp", "replica"),
        P("fsdp", "replica"),
        P("fsdp", "replica"),
    )
    out_specs = (
        P(("replica", "fsdp"), None),
        P(("replica", "fsdp"), None),
        P("replica", "fsdp", None),
        P("replica", "fsdp", None),
        P("replica", "fsdp", None),
        P("fsdp", "replica"),
        P("fsdp", "replica"),
        P("fsdp", "replica"),
    )
    return jax.shard_map(
        on_device, mesh=mesh, in_specs=in_specs, out_specs=out_specs, check_vma=False
    )
```
